32 devices in a mesh: gx: 8 (over y, x, core), gy: 4 (over z).
Axes of the slice: x: 2, y: 2, z: 4, core: 2. Of those that a mesh axis runs over, the one named last changes fastest.
Arguments:
- fields: bfloat16 [10, 32, 512, 512], P(None, None, 'gx', 'gy'), as said below
- dense_list: int32 [4, 8, 10], replicated, may hold values from -1 to 63, as said below
- filter_device: int32 [4, 8, 10], replicated, may hold values from -1 to 7, as said below
- pencil_order: int32 [16], replicated, may hold values from 0 to 15, each once
Outputs:
- tile_stats: float32 [128, 2048], P(('gx', 'gy'))
- coarse_closure: float32 [16, 512], P('gy')
The draws below stay inside these ranges and needn't reach their ends.
Inputs may be any that keep to these rules, and one draw needn't show every extreme that they name: `dense_list`: row [gy, gx] lists distinct local tile indices of device (gx, gy), its listed entries first and -1 after them; in every gy row the busiest device lists 10 tiles and some list only a few. `filter_device`: -1 exactly where dense_list is -1; within a gy row each gx index receives exactly 4 listed tiles and at most 2 from any one listing device, and that most is met. `fields`: channel 0 lies between 0.05 and 0.6; channels 8 and 9 are positive.
All inputs are finite; a program needn't handle non-finite values.
Results may differ from the reference program's by a relative error of at most 0.0003.
Values may be sent and summed in bfloat16 or wider, within the bound.
A program may use at most 192 MiB of HBM per device.

```python
import jax
import jax.numpy as jnp
from jax import lax

TE = 16
HW = 4
CAP = 2
TXD = 4
TYD = 8
TILE_DEV = 64
NX = 512
NY = 512
NZ = 32
DLIST = 10
DMEAN = 4
CXN = 16
NPEN = 16
SUB = 64
LSTAT = 2048
N_GX = 8
N_GY = 4


def tile_plan(base_key):
    quarter = N_GX // 4
    heavy_load = CAP - 1
    source_index = jnp.arange(N_GX, dtype=jnp.int32)
    source_load = jnp.where(source_index < quarter, heavy_load, jnp.where(source_index < 2 * quarter, heavy_load // 2, 0)).astype(jnp.int32)

    def one_group(group_key):
        key_set = jax.random.split(group_key, 3 + N_GX)
        row_perm = jax.random.permutation(key_set[0], N_GX)
        column_perm = jax.random.permutation(key_set[1], N_GX)
        extra_ones = (jax.random.permutation(key_set[2], N_GX) < quarter).astype(jnp.int32)
        index_i = jnp.arange(N_GX, dtype=jnp.int32)[:, None]
        index_j = jnp.arange(N_GX, dtype=jnp.int32)[None, :]
        base_counts = source_load[:, None] + extra_ones[(index_i + index_j) % N_GX]
        counts = base_counts[row_perm][:, column_perm]

        def one_source(source_key, count_row):
            sub_keys = jax.random.split(source_key, 2)
            candidate = jnp.arange(N_GX * CAP, dtype=jnp.int32)
            target = candidate // CAP
            is_taken = candidate % CAP < count_row[target]
            ranking = jnp.where(is_taken, 0, N_GX * CAP) + jax.random.permutation(sub_keys[0], N_GX * CAP).astype(jnp.int32)
            chosen_order = jnp.argsort(ranking)[:DLIST]
            is_valid = is_taken[chosen_order]
            targets = jnp.where(is_valid, target[chosen_order], -1)
            tile_ids = jnp.where(is_valid, jax.random.permutation(sub_keys[1], TILE_DEV)[:DLIST].astype(jnp.int32), -1)
            return (tile_ids, targets)
        return jax.vmap(one_source)(key_set[3:], counts)
    group_keys = jax.random.split(base_key, N_GY)
    tile_ids, targets = jax.vmap(one_group)(group_keys)
    return (tile_ids.astype(jnp.int32), targets.astype(jnp.int32))


def draw_dense_list(key, part):
    return tile_plan(jax.random.fold_in(key, 11))[0]


def draw_filter_device(key, part):
    return tile_plan(jax.random.fold_in(key, 11))[1]


def draw_fields(key, part):
    key_set = jax.random.split(key, 16)
    grid_shape = (NZ, NX, NY)
    tile_shape = (NZ // TE, NX // TE, NY // TE)

    def spread_tiles(values):
        return jnp.repeat(jnp.repeat(jnp.repeat(values, TE, 0), TE, 1), TE, 2)
    solid = jax.random.uniform(key_set[0], grid_shape, jnp.float32, 0.05, 0.6)
    strength = spread_tiles(jnp.exp(jax.random.uniform(key_set[1], tile_shape, jnp.float32, jnp.log(0.25), jnp.log(4.0))))

    def noise(number):
        return jax.random.normal(key_set[number], grid_shape, jnp.float32)
    signs = (0.5, 1.0, -1.5)
    deviation = solid - 0.325
    channels = [solid.astype(jnp.bfloat16)]
    gas_speed = [8.0 * signs[direction] * strength * deviation + noise(2 + direction) for direction in range(3)]
    channels = channels + [speed.astype(jnp.bfloat16) for speed in gas_speed]
    channels = channels + [(0.5 * gas_speed[direction] + 0.5 * noise(5 + direction)).astype(jnp.bfloat16) for direction in range(3)]
    channels.append((4.0 * strength * deviation + noise(8)).astype(jnp.bfloat16))
    granular = jnp.exp(jax.random.uniform(key_set[9], grid_shape, jnp.float32, jnp.log(0.1), 0.0))
    channels.append(granular.astype(jnp.bfloat16))
    friction = jnp.exp(jax.random.uniform(key_set[10], grid_shape, jnp.float32, 0.0, jnp.log(10.0))) * solid / 0.3
    channels.append(friction.astype(jnp.bfloat16))
    return jnp.stack(channels, axis=0)


def setup_inputs(seed: int = 0) -> dict:
    splits = jax.random.split(jax.random.key(seed), 5)
    return {
        "fields": draw_fields(jax.random.fold_in(splits[4], 71), 0),
        "dense_list": draw_dense_list(jax.random.fold_in(splits[4], 71), 0),
        "filter_device": draw_filter_device(jax.random.fold_in(splits[4], 71), 0),
        "pencil_order": jax.random.permutation(splits[3], NPEN).astype(jnp.int32),
    }


def prefix_sums(values, axis):
    running = jnp.cumsum(values, axis=axis)
    lead_shape = list(values.shape)
    lead_shape[axis] = 1
    return jnp.concatenate([jnp.zeros(lead_shape, values.dtype), running], axis=axis)


def window_cut(sums, axis, half_width):
    upper = lax.slice_in_dim(sums, HW + half_width + 1, HW + half_width + 1 + TE, axis=axis)
    lower = lax.slice_in_dim(sums, HW - half_width, HW - half_width + TE, axis=axis)
    return (upper - lower) / (2 * half_width + 1)


def closure_terms(smoothed):
    solid_mean = smoothed[0]
    components = []
    for direction in range(3):
        components.append(smoothed[6 + direction] / solid_mean - smoothed[1 + direction])
    for direction in range(3):
        components.append(smoothed[14 + direction] - smoothed[5] * (smoothed[6 + direction] - smoothed[9 + direction]) / solid_mean)
    components.append(smoothed[12] / solid_mean)
    components.append(smoothed[13] / solid_mean - smoothed[4])
    return jnp.stack(components, axis=0)


def reference(fields, dense_list, filter_device, pencil_order):
    group_no = lax.broadcasted_iota(jnp.int32, dense_list.shape, 0)
    source_no = lax.broadcasted_iota(jnp.int32, dense_list.shape, 1)
    entry_no = lax.broadcasted_iota(jnp.int32, dense_list.shape, 2)
    ranking = ((filter_device * N_GY + group_no) * N_GX + source_no) * DLIST + entry_no
    ranking = jnp.where(filter_device >= 0, ranking, N_GX * N_GY * N_GX * DLIST)
    picked = jnp.argsort(ranking.reshape(-1))[: N_GX * N_GY * DMEAN]
    tile_ids = dense_list.reshape(-1)[picked]
    depth_at = tile_ids // (TXD * TYD)
    column_at = source_no.reshape(-1)[picked] * TXD + (tile_ids // TYD) % TXD
    row_at = group_no.reshape(-1)[picked] * TYD + tile_ids % TYD
    offsets = jnp.arange(TE + 2 * HW, dtype=jnp.int32) - HW

    def extract(depth_one, column_one, row_one):
        z_index = (depth_one * TE + offsets) % NZ
        x_index = (column_one * TE + offsets) % NX
        y_index = (row_one * TE + offsets) % NY
        return fields[:, z_index[:, None, None], x_index[None, :, None], y_index[None, None, :]]

    def block_stats(positions):
        cell_values = jax.vmap(extract)(positions[0], positions[1], positions[2]).astype(jnp.float32)
        tile_count = cell_values.shape[0]
        solid = cell_values[:, 0]
        gas_speed = [cell_values[:, 1 + direction] for direction in range(3)]
        grain_speed = [cell_values[:, 4 + direction] for direction in range(3)]
        pressure = cell_values[:, 7]
        granular = cell_values[:, 8]
        friction = cell_values[:, 9]
        quantity_list = [solid] + gas_speed + [pressure, friction]
        quantity_list = quantity_list + [solid * speed for speed in gas_speed]
        quantity_list = quantity_list + [solid * speed for speed in grain_speed]
        quantity_list = quantity_list + [solid * granular, solid * pressure]
        quantity_list = quantity_list + [friction * (gas_speed[direction] - grain_speed[direction]) for direction in range(3)]
        stacked = jnp.stack(quantity_list, axis=0)
        sub_edge = TE // 4
        per_width = []
        for half_width in range(1, HW + 1):
            smoothed = stacked
            for axis in (2, 3, 4):
                smoothed = window_cut(prefix_sums(smoothed, axis), axis, half_width)
            closure = closure_terms(smoothed).reshape(8, tile_count, sub_edge, 4, sub_edge, 4, sub_edge, 4)
            per_width.append(jnp.mean(closure, axis=(3, 5, 7)).reshape(8, tile_count, SUB))
        result = jnp.stack(per_width, axis=0)
        return jnp.transpose(result, (2, 0, 1, 3)).reshape(tile_count, LSTAT)

    positions = (depth_at.reshape(N_GX * N_GY, DMEAN), column_at.reshape(N_GX * N_GY, DMEAN), row_at.reshape(N_GX * N_GY, DMEAN))
    tile_stats = lax.map(block_stats, positions).reshape(N_GX * N_GY * DMEAN, LSTAT)
    tile_means = jnp.mean(tile_stats.reshape(N_GX * N_GY * DMEAN, HW * 8, SUB), axis=2)
    cell_no = (row_at // 2) * CXN + column_at // 2
    cell_sums = jax.ops.segment_sum(tile_means, cell_no, num_segments=NPEN * CXN)
    counts = jax.ops.segment_sum(jnp.ones_like(tile_means[:, 0]), cell_no, num_segments=NPEN * CXN)
    averaged = cell_sums / jnp.maximum(counts, 1.0)[:, None]
    pencil_grid = averaged.reshape(NPEN, CXN * HW * 8)
    return tile_stats, pencil_grid[pencil_order]
```

```python
import functools

import jax
import jax.numpy as jnp
import numpy as np
from jax import lax
from jax.experimental import pallas as pl
from jax.experimental.pallas import tpu as pltpu
from jax.sharding import PartitionSpec as P

TE = 16
HW = 4
CAP = 2
SPAN = TE + 2 * HW
BF = jnp.bfloat16
F32 = jnp.float32
MESH = pl.DeviceIdType.MESH


def dot(a, b):
    return lax.dot_general(a, b, (((1,), (0,)), ((), ())), preferred_element_type=F32)


def window_weights():
    z = np.arange(SPAN)[:, None, None, None]
    w = np.arange(32)[None, :, None, None]
    zo = np.arange(TE)[None, None, :, None]
    yo = np.arange(TE)[None, None, None, :]
    out = []
    for k in range(1, HW + 1):
        m = (np.abs(z - HW - zo) <= k) & (np.abs(w - HW - yo) <= k)
        m = m.reshape(SPAN * 32, TE * TE)
        out.append(np.concatenate([m, m], axis=0))
    return np.stack(out).astype(jnp.bfloat16)


def block_weights():
    par = np.arange(2)[:, None, None, None]
    bx = np.arange(4)[None, :, None, None]
    h = np.arange(2)[None, None, :, None]
    lane = np.arange(128)[None, None, None, :]
    plane = h * 128 + lane
    target = par * 64 + (plane // TE // 4) * 16 + bx * 4 + (plane % TE) // 4
    target = target.reshape(-1)
    m = (target[:, None] == np.arange(128)[None, :]) / 64.0
    return np.concatenate([m, m], axis=0).astype(jnp.bfloat16)


def edge_weights(nz):
    z = np.arange(nz)[:, None, None, None]
    r = np.arange(HW)[None, :, None, None]
    zs = np.arange(nz)[None, None, :, None]
    s = np.arange(16)[None, None, None, :]
    last = ((z == zs) & (s == 12 + r)).reshape(nz * HW, nz * 16)
    first = ((z == zs) & (s == r)).reshape(nz * HW, nz * 16)
    take = np.stack([last, first])
    give = np.stack([last.T, first.T])
    return take.astype(jnp.bfloat16), give.astype(jnp.bfloat16)


def column_weights(nz, ny):
    z = np.arange(nz)[:, None, None, None]
    y = np.arange(ny)[None, :, None, None]
    side = np.arange(2)[None, None, :, None]
    lane = np.arange(128)[None, None, None, :]
    low = (side == 0) & (y >= ny - HW) & (lane == z * HW + y - (ny - HW))
    high = (side == 1) & (y < HW) & (lane == z * HW + y)
    return (low | high).reshape(nz // 2, 2 * ny, 256).astype(jnp.bfloat16)


def halo_kernel(
    gxn, gyn, f_ref, take_ref, give_ref, col_ref, p_ref, yh_ref, sx, rx, sy, ssem, rsem
):
    nc, nz, nx, ny = f_ref.shape
    px = nx + 32
    gx, gy = lax.axis_index("gx"), lax.axis_index("gy")
    right = (lax.rem(gx + 1, gxn), gy)
    left = (lax.rem(gx + gxn - 1, gxn), gy)
    up = (gx, lax.rem(gy + 1, gyn))
    down = (gx, lax.rem(gy + gyn - 1, gyn))
    barrier = pltpu.get_barrier_semaphore()
    for who in (left, right, up, down):
        pl.semaphore_signal(barrier, inc=1, device_id=who, device_id_type=MESH)
    hz = nz * HW
    for side, start in ((0, nx - 16), (1, 0)):
        for c in range(nc):
            block = f_ref[c, :, start : start + 16, :].reshape(nz * 16, ny)
            sx[side, c * hz : (c + 1) * hz, :] = dot(take_ref[side], block).astype(BF)
    pl.semaphore_wait(barrier, 4)
    copies = []
    for side, who in ((0, right), (1, left)):
        copies.append(
            pltpu.make_async_remote_copy(
                src_ref=sx.at[side],
                dst_ref=rx.at[side],
                send_sem=ssem.at[side],
                recv_sem=rsem.at[side],
                device_id=who,
                device_id_type=MESH,
            )
        )
        copies[-1].start()

    def pack(lo, rows):
        acc = None
        for j in range(nz // 2):
            lhs = jnp.concatenate(
                [
                    p_ref[:, 2 * j + i, lo : lo + rows, :].reshape(nc * rows, ny)
                    for i in range(2)
                ],
                axis=1,
            )
            part = dot(lhs, col_ref[j])
            acc = part if acc is None else acc + part
        for side in range(2):
            sy[side, :, lo : lo + rows, :] = (
                acc[:, side * 128 : (side + 1) * 128].astype(BF).reshape(nc, rows, 128)
            )

    for c in range(nc):
        p_ref[c, :, 16 : 16 + nx, :] = f_ref[c]
    for part in range(nx // 16):
        pack(16 + 16 * part, 16)
    for side, start in ((0, 0), (1, px - 16)):
        copies[side].wait()
        for c in range(nc):
            block = dot(give_ref[side], rx[side, c * hz : (c + 1) * hz, :])
            p_ref[c, :, start : start + 16, :] = block.astype(BF).reshape(nz, 16, ny)
    pack(0, 16)
    pack(px - 16, 16)
    copies = []
    for side, who in ((0, up), (1, down)):
        copies.append(
            pltpu.make_async_remote_copy(
                src_ref=sy.at[side],
                dst_ref=yh_ref.at[side],
                send_sem=ssem.at[2 + side],
                recv_sem=rsem.at[2 + side],
                device_id=who,
                device_id_type=MESH,
            )
        )
        copies[-1].start()
    for copy in copies:
        copy.wait()


def iota(shape, dim):
    return lax.broadcasted_iota(jnp.int32, shape, dim)


def one_hot(cond):
    return jnp.where(cond, 1.0, 0.0).astype(BF)


def tile_kernel(
    gxn,
    gyn,
    list_length,
    list_ref,
    target_ref,
    p_ref,
    yh_ref,
    w_ref,
    m_ref,
    pay_ref,
    t_ref,
    qp_ref,
    qm_ref,
    r_ref,
    c_ref,
    a_ref,
    s_ref,
    cell_ref,
    count_ref,
    used_ref,
):
    nc, nz, px, ny = p_ref.shape
    across_x, across_y = (px - 32) // TE, ny // TE
    base = (lax.axis_index("gy") * gxn + lax.axis_index("gx")) * list_length
    total = jnp.int32(0)
    for e in range(list_length):
        total = total + jnp.where(target_ref[base + e] >= 0, 1, 0).astype(jnp.int32)
    quads = SPAN // 4

    @pl.loop(0, total)
    def _(t):
        tile = list_ref[base + t]
        tz = tile // (across_x * across_y)
        lx = tile // across_y % across_x
        ly = tile % across_y
        row = iota((4 * ny, 128), 0)
        col = iota((4 * ny, 128), 1)
        w = col % 32
        spread = one_hot(
            (row // ny == col // 32) & (w < SPAN) & (row % ny == ly * TE - HW + w)
        )
        x0 = pl.multiple_of(lx * TE, TE)
        for j in range(quads):
            z0 = (tz * TE - HW + 4 * j + nz) % nz
            lhs = jnp.concatenate(
                [
                    p_ref[:, z0 + i, pl.ds(x0, 48), :].reshape(nc * 48, ny)
                    for i in range(4)
                ],
                axis=1,
            )
            t_ref[j] = dot(lhs, spread)

        @pl.when((ly == 0) | (ly == across_y - 1))
        def _():
            lhs = jnp.concatenate(
                [yh_ref[side, :, pl.ds(x0, 48), :].reshape(nc * 48, 128) for side in range(2)],
                axis=1,
            )
            lane = iota((256, 128), 0)
            out = iota((256, 128), 1)
            ww = out % 32
            for j in range(quads):
                z0 = (tz * TE - HW + 4 * j + nz) % nz
                source = (z0 + out // 32) * HW
                low = (ly == 0) & (ww < HW) & (lane == source + ww)
                high = (
                    (ly == across_y - 1)
                    & (ww >= SPAN - HW)
                    & (ww < SPAN)
                    & (lane == 128 + source + ww - (SPAN - HW))
                )
                t_ref[j] = t_ref[j] + dot(lhs, one_hot(low | high))

        for j in range(quads):
            lanes = slice(j * 128, (j + 1) * 128)
            lanes_low = slice((quads + j) * 128, (quads + j + 1) * 128)
            v = [t_ref[j, c * 48 + 12 : c * 48 + 36, :] for c in range(nc)]
            plain = [v[0], v[1], v[2], v[3], v[7], v[9]]
            for i in range(3):
                pair = jnp.concatenate(plain[2 * i : 2 * i + 2], axis=0)
                qp_ref[i * 48 : i * 48 + 48, lanes] = pair.astype(BF)
            prods = [v[0] * v[c] for c in (1, 2, 3, 4, 5, 6, 8, 7)]
            prods = prods + [v[9] * (v[1 + d] - v[4 + d]) for d in range(3)]
            for i in range(6):
                if i < 5:
                    pair = jnp.concatenate(prods[2 * i : 2 * i + 2], axis=0)
                else:
                    pair = jnp.concatenate([prods[10], jnp.zeros((8, 128), F32)], axis=0)
                rows = slice(i * 48, i * 48 + pair.shape[0])
                high = pair.astype(BF)
                qm_ref[rows, lanes] = high
                qm_ref[rows, lanes_low] = (pair - high.astype(F32)).astype(BF)
        for k in range(1, HW + 1):
            rp = dot(qp_ref[...], w_ref[k - 1, : SPAN * 32, :])
            rm = dot(qm_ref[...], w_ref[k - 1])
            scale = 1.0 / (2 * k + 1) ** 3
            for h in range(2):
                r_ref[k - 1, h, :144, :] = rp[:, h * 128 : (h + 1) * 128]
                r_ref[k - 1, h, 144:, :] = rm[:, h * 128 : (h + 1) * 128]
            for h in range(2):

                def f(q):
                    acc = None
                    for d in range(-k, k + 1):
                        start = q * SPAN + HW + d
                        part = r_ref[k - 1, h, start : start + TE, :]
                        acc = part if acc is None else acc + part
                    return acc

                inv = 1.0 / f(0)
                drag = f(5) * scale
                comps = [None] * 8
                for d in range(3):
                    ag = f(6 + d)
                    comps[d] = ag * inv - f(1 + d) * scale
                    comps[3 + d] = f(14 + d) * scale - drag * ((ag - f(9 + d)) * inv)
                comps[6] = f(12) * inv
                comps[7] = f(13) * inv - f(4) * scale
                for i in range(8):
                    at = ((k - 1) * 8 + i) * TE
                    c_ref[h, at : at + TE, :] = comps[i]
        where = pl.ds(pl.multiple_of(t * 16, 16), 16)
        for par in range(2):
            for bx in range(4):
                for h in range(2):
                    acc = None
                    for r in range(4):
                        part = c_ref[h, pl.ds(par * TE + bx * 4 + r, 16, stride=2 * TE), :]
                        acc = part if acc is None else acc + part
                    at = ((par * 4 + bx) * 2 + h) * 128
                    high = acc.astype(BF)
                    a_ref[where, at : at + 128] = high
                    a_ref[where, 2048 + at : 2048 + at + 128] = (
                        acc - high.astype(F32)
                    ).astype(BF)

    s_ref[...] = dot(a_ref[...], m_ref[...])
    cells = cell_ref.shape[0]
    cell_ref[...] = jnp.zeros(cell_ref.shape, F32)
    count_ref[...] = jnp.zeros(count_ref.shape, F32)
    for g in range(gxn):
        used_ref[g] = 0

    @pl.loop(0, total)
    def _(t):
        tile = list_ref[base + t]
        lx = tile // across_y % across_x
        ly = tile % across_y
        cell = (ly // 2) * (across_x // 2) + lx // 2
        target = target_ref[base + t]
        rank = used_ref[target]
        used_ref[target] = rank + 1
        stats = s_ref[pl.ds(pl.multiple_of(t * 16, 16), 16), :]
        pay_ref[target, pl.ds(pl.multiple_of(rank * 16, 16), 16), :] = stats
        cell_ref[cell] = cell_ref[cell] + stats
        count_ref[cell] = count_ref[cell] + 1.0

    lane = iota((16, 128), 1)
    row = iota((16, 128), 0)
    rows = []
    for cell in range(cells):
        sums = cell_ref[cell]
        even = jnp.sum(jnp.where(lane < 64, sums, 0.0), axis=1, keepdims=True)
        odd = jnp.sum(jnp.where(lane >= 64, sums, 0.0), axis=1, keepdims=True)
        spot = lane % 32
        placed = jnp.where(spot == 2 * row, even, jnp.where(spot == 2 * row + 1, odd, 0.0))
        sums = jnp.sum(placed, axis=0, keepdims=True) * (1.0 / 64.0)
        rows.append(sums / jnp.maximum(count_ref[cell, 0:1, :], 1.0))
    coarse = jnp.concatenate(rows, axis=0)
    for g in range(gxn):
        pay_ref[g, CAP * 16 : CAP * 16 + cells, :] = coarse


def exchange_kernel(gxn, gyn, pay_ref, got_ref, all_ref, mine, xs, xr, ys, yr):
    gx, gy = lax.axis_index("gx"), lax.axis_index("gy")
    barrier = pltpu.get_barrier_semaphore()
    for d in range(1, gxn):
        pl.semaphore_signal(
            barrier, inc=1, device_id=(lax.rem(gx + d, gxn), gy), device_id_type=MESH
        )
    for d in range(1, gyn):
        pl.semaphore_signal(
            barrier, inc=1, device_id=(gx, lax.rem(gy + d, gyn)), device_id_type=MESH
        )
    pl.semaphore_wait(barrier, gxn + gyn - 2)
    copies = []
    for d in range(1, gxn):
        who = lax.rem(gx + d, gxn)
        copies.append(
            pltpu.make_async_remote_copy(
                src_ref=pay_ref.at[who],
                dst_ref=got_ref.at[gx],
                send_sem=xs.at[d],
                recv_sem=xr.at[d],
                device_id=(who, gy),
                device_id_type=MESH,
            )
        )
        copies[-1].start()
    got_ref[gx] = pay_ref[gx]
    for copy in copies:
        copy.wait()
    cells = mine.shape[1]
    for g in range(gxn):
        mine[g] = got_ref[g, CAP * 16 : CAP * 16 + cells, :]
    copies = []
    for d in range(1, gyn):
        copies.append(
            pltpu.make_async_remote_copy(
                src_ref=mine,
                dst_ref=all_ref.at[gy],
                send_sem=ys.at[d],
                recv_sem=yr.at[d],
                device_id=(gx, lax.rem(gy + d, gyn)),
                device_id_type=MESH,
            )
        )
        copies[-1].start()
    all_ref[gy] = mine[...]
    for copy in copies:
        copy.wait()


def select_kernel(
    gxn, gyn, list_length, cells_x, target_ref, order_ref, got_ref, all_ref, o_ref, c_ref
):
    gx, gy = lax.axis_index("gx"), lax.axis_index("gy")

    def source(s, slot):
        def entry(e, carry):
            slot, rank = carry
            hit = target_ref[(gy * gxn + s) * list_length + e] == gx

            @pl.when(hit)
            def _():
                at = pl.multiple_of(rank * 16, 16)
                o_ref[slot] = got_ref[s, pl.ds(at, 16), :]

            step = jnp.where(hit, 1, 0).astype(jnp.int32)
            return slot + step, rank + step

        return lax.fori_loop(0, list_length, entry, (slot, jnp.int32(0)))[0]

    lax.fori_loop(0, gxn, source, jnp.int32(0))
    per_row = c_ref.shape[0]
    cells_y = all_ref.shape[2] // cells_x
    group = iota((1, 128), 1) // 32
    for r in range(per_row):
        pencil = order_ref[gy * per_row + r]
        owner = pencil // cells_y
        first = pencil % cells_y * cells_x
        for part in range(c_ref.shape[1] // 128):
            row = None
            for i in range(4):
                cx = part * 4 + i
                value = all_ref[owner, cx // cells_x, pl.ds(first + cx % cells_x, 1), :]
                row = value if row is None else jnp.where(group == i, value, row)
            c_ref[r : r + 1, part * 128 : (part + 1) * 128] = row


VM = pl.BlockSpec(memory_space=pltpu.VMEM)
SM = pl.BlockSpec(memory_space=pltpu.SMEM)


def shards(gxn, gyn, fields, dense_list, filter_device, pencil_order):
    nc, nz, nx, ny = fields.shape
    list_length = dense_list.shape[2]
    per_filter = gxn // 4 * (CAP + (CAP - 1) // 2)
    cells_x = nx // TE // 2
    cells = cells_x * (ny // TE // 2)
    pencils = pencil_order.shape[0]
    px = nx + 32
    take, give = edge_weights(nz)
    padded, columns = pl.pallas_call(
        functools.partial(halo_kernel, gxn, gyn),
        out_shape=(
            jax.ShapeDtypeStruct((nc, nz, px, ny), BF),
            jax.ShapeDtypeStruct((2, nc, px, 128), BF),
        ),
        in_specs=[VM] * 4,
        out_specs=(VM, VM),
        scratch_shapes=[
            pltpu.VMEM((2, nc * nz * HW, ny), BF),
            pltpu.VMEM((2, nc * nz * HW, ny), BF),
            pltpu.VMEM((2, nc, px, 128), BF),
            pltpu.SemaphoreType.DMA((4,)),
            pltpu.SemaphoreType.DMA((4,)),
        ],
        compiler_params=pltpu.CompilerParams(
            collective_id=0, has_side_effects=True, vmem_limit_bytes=40 << 20
        ),
        name="halo",
    )(fields, jnp.asarray(take), jnp.asarray(give), jnp.asarray(column_weights(nz, ny)))
    lists = dense_list.reshape(-1)
    targets = filter_device.reshape(-1)
    payload = pl.pallas_call(
        functools.partial(tile_kernel, gxn, gyn, list_length),
        out_shape=jax.ShapeDtypeStruct((gxn, CAP * 16 + cells, 128), F32),
        in_specs=[SM, SM, VM, VM, VM, VM],
        out_specs=VM,
        scratch_shapes=[
            pltpu.VMEM((SPAN // 4, nc * 48, 128), F32),
            pltpu.VMEM((144, SPAN * 32), BF),
            pltpu.VMEM((272, 2 * SPAN * 32), BF),
            pltpu.VMEM((HW, 2, 416, 128), F32),
            pltpu.VMEM((2, HW * 8 * TE, 128), F32),
            pltpu.VMEM((list_length * 16, 4096), BF),
            pltpu.VMEM((list_length * 16, 128), F32),
            pltpu.VMEM((cells, 16, 128), F32),
            pltpu.VMEM((cells, 8, 128), F32),
            pltpu.SMEM((gxn,), jnp.int32),
        ],
        compiler_params=pltpu.CompilerParams(vmem_limit_bytes=40 << 20),
        name="tiles",
    )(
        lists,
        targets,
        padded,
        columns,
        jnp.asarray(window_weights()),
        jnp.asarray(block_weights()),
    )
    got, every = pl.pallas_call(
        functools.partial(exchange_kernel, gxn, gyn),
        out_shape=(
            jax.ShapeDtypeStruct(payload.shape, F32),
            jax.ShapeDtypeStruct((gyn, gxn, cells, 128), F32),
        ),
        in_specs=[VM],
        out_specs=(VM, VM),
        scratch_shapes=[
            pltpu.VMEM((gxn, cells, 128), F32),
            pltpu.SemaphoreType.DMA((gxn,)),
            pltpu.SemaphoreType.DMA((gxn,)),
            pltpu.SemaphoreType.DMA((gyn,)),
            pltpu.SemaphoreType.DMA((gyn,)),
        ],
        compiler_params=pltpu.CompilerParams(collective_id=1, has_side_effects=True),
        name="exchange",
    )(payload)
    statistics, coarse = pl.pallas_call(
        functools.partial(select_kernel, gxn, gyn, list_length, cells_x),
        out_shape=(
            jax.ShapeDtypeStruct((per_filter, 16, 128), F32),
            jax.ShapeDtypeStruct((pencils // gyn, cells_x * gxn * HW * 8), F32),
        ),
        in_specs=[SM, SM, VM, VM],
        out_specs=(VM, VM),
        name="select",
    )(targets, pencil_order, got, every)
    return statistics.reshape(per_filter, 2048), coarse


def solution(mesh):
    in_specs = (P(None, None, "gx", "gy"), P(), P(), P())
    out_specs = (P(("gx", "gy"), None), P("gy", None))
    body = functools.partial(shards, mesh.shape["gx"], mesh.shape["gy"])
    return jax.shard_map(
        body, mesh=mesh, in_specs=in_specs, out_specs=out_specs, check_vma=False
    )
```

```python
import functools

import jax
import jax.numpy as jnp
import numpy as np
from jax import lax
from jax.experimental import pallas as pl
from jax.experimental.pallas import tpu as pltpu
from jax.sharding import PartitionSpec as P

TE = 16
HW = 4
CAP = 2
SPAN = TE + 2 * HW
BF = jnp.bfloat16
F32 = jnp.float32
MESH = pl.DeviceIdType.MESH


def dot(a, b):
    return lax.dot_general(a, b, (((1,), (0,)), ((), ())), preferred_element_type=F32)


def window_weights():
    z = np.arange(SPAN)[:, None, None, None]
    w = np.arange(32)[None, :, None, None]
    zo = np.arange(TE)[None, None, :, None]
    yo = np.arange(TE)[None, None, None, :]
    out = []
    for k in range(1, HW + 1):
        m = (np.abs(z - HW - zo) <= k) & (np.abs(w - HW - yo) <= k)
        m = m.reshape(SPAN * 32, TE * TE)
        out.append(np.concatenate([m, m], axis=0))
    return np.stack(out).astype(jnp.bfloat16)


def block_weights():
    par = np.arange(2)[:, None, None, None]
    bx = np.arange(4)[None, :, None, None]
    h = np.arange(2)[None, None, :, None]
    lane = np.arange(128)[None, None, None, :]
    plane = h * 128 + lane
    target = par * 64 + (plane // TE // 4) * 16 + bx * 4 + (plane % TE) // 4
    target = target.reshape(-1)
    m = (target[:, None] == np.arange(128)[None, :]) / 64.0
    return np.concatenate([m, m], axis=0).astype(jnp.bfloat16)


def halo_kernel(gxn, gyn, f_ref, e_ref, yh_ref, yc_ref, col, sx, rx, sy, sc, ssem, rsem):
    nc, nz, nx, ny = f_ref.shape
    gx, gy = lax.axis_index("gx"), lax.axis_index("gy")
    right = (lax.rem(gx + 1, gxn), gy)
    left = (lax.rem(gx + gxn - 1, gxn), gy)
    up = (gx, lax.rem(gy + 1, gyn))
    down = (gx, lax.rem(gy + gyn - 1, gyn))
    barrier = pltpu.get_barrier_semaphore()
    for who in (left, right, up, down):
        pl.semaphore_signal(barrier, inc=1, device_id=who, device_id_type=MESH)
    hz = nz * HW

    def send(src, dst, sem, who):
        copy = pltpu.make_async_remote_copy(
            src_ref=src,
            dst_ref=dst,
            send_sem=ssem.at[sem],
            recv_sem=rsem.at[sem],
            device_id=who,
            device_id_type=MESH,
        )
        copy.start()
        return copy

    row = iota((2 * ny, 256), 0)
    lane = iota((2 * ny, 256), 1)
    y, l = row % ny, lane % 128
    spot = l - row // ny * HW
    low = jnp.where((lane < 128) & (y >= ny - HW), spot - y + (ny - HW), -1)
    base = jnp.where((lane >= 128) & (y < HW), spot - y, low)
    for j in range(nz // 2):
        col[j] = one_hot(base == 2 * HW * j)

    def pack(ref, lo):
        acc = None
        for j in range(nz // 2):
            lhs = jnp.concatenate(
                [ref[:, 2 * j + i, lo : lo + 16, :].reshape(nc * 16, ny) for i in range(2)],
                axis=1,
            )
            part = dot(lhs, col[j])
            acc = part if acc is None else acc + part
        return [
            acc[:, side * 128 : (side + 1) * 128].astype(BF).reshape(nc, 16, 128)
            for side in range(2)
        ]

    out = iota((hz, nz * 16), 0)
    put = iota((hz, nz * 16), 1)
    same = out // HW == put // 16
    pl.semaphore_wait(barrier, 4)
    xcopies = []
    for side, start, first, who in ((0, nx - 16, 16 - HW, right), (1, 0, 0, left)):
        take = one_hot(same & (put % 16 == first + out % HW))
        for c in range(nc):
            block = f_ref[c, :, start : start + 16, :].reshape(nz * 16, ny)
            sx[side, c * hz : (c + 1) * hz, :] = dot(take, block).astype(BF)
        xcopies.append(send(sx.at[side], rx.at[side], side, who))
    for part in range(nx // 16):
        both = pack(f_ref, part * 16)
        for side in range(2):
            sy[side, :, part * 16 : part * 16 + 16, :] = both[side]
    ycopies = [send(sy.at[0], yh_ref.at[0], 2, up), send(sy.at[1], yh_ref.at[1], 3, down)]
    put = iota((nz * 16, 2 * hz), 0)
    src = iota((nz * 16, 2 * hz), 1)
    code = put - put // 16 * 16
    inner = src % hz
    give = one_hot(
        (put // 16 == inner // HW)
        & (code == inner % HW + jnp.where(src < hz, 16 - HW, 0))
    )
    for copy in xcopies:
        copy.wait()
    for c in range(nc):
        rows = slice(c * hz, (c + 1) * hz)
        block = dot(give, jnp.concatenate([rx[0, rows, :], rx[1, rows, :]], axis=0))
        e_ref[c] = block.astype(BF).reshape(nz, 16, ny)
    both = pack(e_ref, 0)
    for side in range(2):
        sc[side] = both[side]
    ycopies.append(send(sc.at[0], yc_ref.at[0], 4, up))
    ycopies.append(send(sc.at[1], yc_ref.at[1], 5, down))
    for copy in ycopies:
        copy.wait()


def iota(shape, dim):
    return lax.broadcasted_iota(jnp.int32, shape, dim)


def one_hot(cond):
    return jnp.where(cond, 1.0, 0.0).astype(BF)


def tile_kernel(
    gxn,
    gyn,
    list_length,
    list_ref,
    target_ref,
    f_ref,
    e_ref,
    yh_ref,
    yc_ref,
    w_ref,
    m_ref,
    pay_ref,
    t_ref,
    qp_ref,
    qm_ref,
    r_ref,
    c_ref,
    a_ref,
    s_ref,
    cell_ref,
    count_ref,
    used_ref,
):
    nc, nz, nx, ny = f_ref.shape
    across_x, across_y = nx // TE, ny // TE
    gx, gy = lax.axis_index("gx"), lax.axis_index("gy")
    total = jnp.int32(0)
    for e in range(list_length):
        total = total + jnp.where(target_ref[gy, gx, e] >= 0, 1, 0).astype(jnp.int32)
    quads = SPAN // 4

    @pl.loop(0, total)
    def _(t):
        tile = list_ref[gy, gx, t]
        tz = tile // (across_x * across_y)
        lx = tile // across_y % across_x
        ly = tile % across_y
        row = iota((4 * ny, 128), 0)
        col = iota((4 * ny, 128), 1)
        w = col % 32
        spread = one_hot(
            (row // ny == col // 32) & (w < SPAN) & (row % ny == ly * TE - HW + w)
        )
        x0 = pl.multiple_of(lx * TE, TE)
        x_low = pl.multiple_of(jnp.maximum(lx - 1, 0) * TE, TE)
        x_high = pl.multiple_of(jnp.minimum(lx + 1, across_x - 1) * TE, TE)

        def three(own, edge):
            low = jnp.where(lx == 0, edge, own(x_low))
            high = jnp.where(lx == across_x - 1, edge, own(x_high))
            return jnp.concatenate([low, own(x0), high], axis=1).reshape(nc * 48, 128)

        for j in range(quads):
            z0 = (tz * TE - HW + 4 * j + nz) % nz
            lhs = jnp.concatenate(
                [
                    three(lambda x, i=i: f_ref[:, z0 + i, pl.ds(x, 16), :], e_ref[:, z0 + i])
                    for i in range(4)
                ],
                axis=1,
            )
            t_ref[j] = dot(lhs, spread)

        @pl.when((ly == 0) | (ly == across_y - 1))
        def _():
            lhs = jnp.concatenate(
                [three(lambda x, i=i: yh_ref[i, :, pl.ds(x, 16), :], yc_ref[i]) for i in range(2)],
                axis=1,
            )
            lane = iota((256, 128), 0)
            out = iota((256, 128), 1)
            ww = out % 32
            for j in range(quads):
                z0 = (tz * TE - HW + 4 * j + nz) % nz
                source = (z0 + out // 32) * HW
                low = (ly == 0) & (ww < HW) & (lane == source + ww)
                high = (
                    (ly == across_y - 1)
                    & (ww >= SPAN - HW)
                    & (ww < SPAN)
                    & (lane == 128 + source + ww - (SPAN - HW))
                )
                t_ref[j] = t_ref[j] + dot(lhs, one_hot(low | high))

        for j in range(quads):
            lanes = slice(j * 128, (j + 1) * 128)
            lanes_low = slice((quads + j) * 128, (quads + j + 1) * 128)
            v = [t_ref[j, c * 48 + 12 : c * 48 + 36, :] for c in range(nc)]
            plain = [v[0], v[1], v[2], v[3], v[7], v[9]]
            for i in range(3):
                pair = jnp.concatenate(plain[2 * i : 2 * i + 2], axis=0)
                qp_ref[i * 48 : i * 48 + 48, lanes] = pair.astype(BF)
            prods = [v[0] * v[c] for c in (1, 2, 3, 4, 5, 6, 8, 7)]
            prods = prods + [v[9] * (v[1 + d] - v[4 + d]) for d in range(3)]
            for i in range(6):
                if i < 5:
                    pair = jnp.concatenate(prods[2 * i : 2 * i + 2], axis=0)
                else:
                    pair = jnp.concatenate([prods[10], jnp.zeros((8, 128), F32)], axis=0)
                rows = slice(i * 48, i * 48 + pair.shape[0])
                high = pair.astype(BF)
                qm_ref[rows, lanes] = high
                qm_ref[rows, lanes_low] = (pair - high.astype(F32)).astype(BF)
        for k in range(1, HW + 1):
            rp = dot(qp_ref[...], w_ref[k - 1, : SPAN * 32, :])
            rm = dot(qm_ref[...], w_ref[k - 1])
            scale = 1.0 / (2 * k + 1) ** 3
            for h in range(2):
                r_ref[k - 1, h, :144, :] = rp[:, h * 128 : (h + 1) * 128]
                r_ref[k - 1, h, 144:, :] = rm[:, h * 128 : (h + 1) * 128]
            for h in range(2):

                def f(q):
                    acc = None
                    for d in range(-k, k + 1):
                        start = q * SPAN + HW + d
                        part = r_ref[k - 1, h, start : start + TE, :]
                        acc = part if acc is None else acc + part
                    return acc

                inv = 1.0 / f(0)
                drag = f(5) * scale
                comps = [None] * 8
                for d in range(3):
                    ag = f(6 + d)
                    comps[d] = ag * inv - f(1 + d) * scale
                    comps[3 + d] = f(14 + d) * scale - drag * ((ag - f(9 + d)) * inv)
                comps[6] = f(12) * inv
                comps[7] = f(13) * inv - f(4) * scale
                for i in range(8):
                    at = ((k - 1) * 8 + i) * TE
                    c_ref[h, at : at + TE, :] = comps[i]
        where = pl.ds(pl.multiple_of(t * 16, 16), 16)
        for par in range(2):
            for bx in range(4):
                for h in range(2):
                    acc = None
                    for r in range(4):
                        part = c_ref[h, pl.ds(par * TE + bx * 4 + r, 16, stride=2 * TE), :]
                        acc = part if acc is None else acc + part
                    at = ((par * 4 + bx) * 2 + h) * 128
                    high = acc.astype(BF)
                    a_ref[where, at : at + 128] = high
                    a_ref[where, 2048 + at : 2048 + at + 128] = (
                        acc - high.astype(F32)
                    ).astype(BF)

    s_ref[...] = dot(a_ref[...], m_ref[...])
    cells = cell_ref.shape[0]
    cell_ref[...] = jnp.zeros(cell_ref.shape, F32)
    count_ref[...] = jnp.zeros(count_ref.shape, F32)
    for g in range(gxn):
        used_ref[g] = 0

    @pl.loop(0, total)
    def _(t):
        tile = list_ref[gy, gx, t]
        lx = tile // across_y % across_x
        ly = tile % across_y
        cell = (ly // 2) * (across_x // 2) + lx // 2
        target = target_ref[gy, gx, t]
        rank = used_ref[target]
        used_ref[target] = rank + 1
        stats = s_ref[pl.ds(pl.multiple_of(t * 16, 16), 16), :]
        pay_ref[target, pl.ds(pl.multiple_of(rank * 16, 16), 16), :] = stats
        cell_ref[cell] = cell_ref[cell] + stats
        count_ref[cell] = count_ref[cell] + 1.0

    lane = iota((16, 128), 1)
    row = iota((16, 128), 0)
    rows = []
    for cell in range(cells):
        sums = cell_ref[cell]
        even = jnp.sum(jnp.where(lane < 64, sums, 0.0), axis=1, keepdims=True)
        odd = jnp.sum(jnp.where(lane >= 64, sums, 0.0), axis=1, keepdims=True)
        spot = lane % 32
        placed = jnp.where(spot == 2 * row, even, jnp.where(spot == 2 * row + 1, odd, 0.0))
        sums = jnp.sum(placed, axis=0, keepdims=True) * (1.0 / 64.0)
        rows.append(sums / jnp.maximum(count_ref[cell, 0:1, :], 1.0))
    coarse = jnp.concatenate(rows, axis=0)
    for g in range(gxn):
        pay_ref[g, CAP * 16 : CAP * 16 + cells, :] = coarse


def exchange_kernel(gxn, gyn, pay_ref, got_ref, all_ref, mine, xs, xr, ys, yr):
    gx, gy = lax.axis_index("gx"), lax.axis_index("gy")
    barrier = pltpu.get_barrier_semaphore()
    for d in range(1, gxn):
        pl.semaphore_signal(
            barrier, inc=1, device_id=(lax.rem(gx + d, gxn), gy), device_id_type=MESH
        )
    for d in range(1, gyn):
        pl.semaphore_signal(
            barrier, inc=1, device_id=(gx, lax.rem(gy + d, gyn)), device_id_type=MESH
        )
    pl.semaphore_wait(barrier, gxn + gyn - 2)
    copies = []
    for d in range(1, gxn):
        who = lax.rem(gx + d, gxn)
        copies.append(
            pltpu.make_async_remote_copy(
                src_ref=pay_ref.at[who],
                dst_ref=got_ref.at[gx],
                send_sem=xs.at[d],
                recv_sem=xr.at[d],
                device_id=(who, gy),
                device_id_type=MESH,
            )
        )
        copies[-1].start()
    got_ref[gx] = pay_ref[gx]
    for copy in copies:
        copy.wait()
    cells = mine.shape[1]
    for g in range(gxn):
        mine[g] = got_ref[g, CAP * 16 : CAP * 16 + cells, :]
    copies = []
    for d in range(1, gyn):
        copies.append(
            pltpu.make_async_remote_copy(
                src_ref=mine,
                dst_ref=all_ref.at[gy],
                send_sem=ys.at[d],
                recv_sem=yr.at[d],
                device_id=(gx, lax.rem(gy + d, gyn)),
                device_id_type=MESH,
            )
        )
        copies[-1].start()
    all_ref[gy] = mine[...]
    for copy in copies:
        copy.wait()


def select_kernel(
    gxn, gyn, list_length, cells_x, target_ref, order_ref, got_ref, all_ref, o_ref, c_ref, held
):
    gx, gy = lax.axis_index("gx"), lax.axis_index("gy")

    def source(s, slot):
        def entry(e, carry):
            slot, rank = carry
            hit = target_ref[gy, s, e] == gx

            @pl.when(hit)
            def _():
                at = pl.multiple_of(rank * 16, 16)
                held[slot] = got_ref[s, pl.ds(at, 16), :]

            step = jnp.where(hit, 1, 0).astype(jnp.int32)
            return slot + step, rank + step

        return lax.fori_loop(0, list_length, entry, (slot, jnp.int32(0)))[0]

    lax.fori_loop(0, gxn, source, jnp.int32(0))
    for slot in range(o_ref.shape[0]):
        for r in range(16):
            o_ref[slot : slot + 1, r * 128 : (r + 1) * 128] = held[slot, r : r + 1, :]
    per_row = c_ref.shape[0]
    cells_y = all_ref.shape[2] // cells_x
    group = iota((1, 128), 1) // 32
    for r in range(per_row):
        pencil = order_ref[gy * per_row + r]
        owner = pencil // cells_y
        first = pencil % cells_y * cells_x
        for part in range(c_ref.shape[1] // 128):
            row = None
            for i in range(4):
                cx = part * 4 + i
                value = all_ref[owner, cx // cells_x, pl.ds(first + cx % cells_x, 1), :]
                row = value if row is None else jnp.where(group == i, value, row)
            c_ref[r : r + 1, part * 128 : (part + 1) * 128] = row


VM = pl.BlockSpec(memory_space=pltpu.VMEM)
SM = pl.BlockSpec(memory_space=pltpu.SMEM)


def shards(gxn, gyn, fields, dense_list, filter_device, pencil_order):
    nc, nz, nx, ny = fields.shape
    list_length = dense_list.shape[2]
    per_filter = gxn // 4 * (CAP + (CAP - 1) // 2)
    cells_x = nx // TE // 2
    cells = cells_x * (ny // TE // 2)
    pencils = pencil_order.shape[0]
    edges, columns, corners = pl.pallas_call(
        functools.partial(halo_kernel, gxn, gyn),
        out_shape=(
            jax.ShapeDtypeStruct((nc, nz, 16, ny), BF),
            jax.ShapeDtypeStruct((2, nc, nx, 128), BF),
            jax.ShapeDtypeStruct((2, nc, 16, 128), BF),
        ),
        in_specs=[VM],
        out_specs=(VM, VM, VM),
        scratch_shapes=[
            pltpu.VMEM((nz // 2, 2 * ny, 256), BF),
            pltpu.VMEM((2, nc * nz * HW, ny), BF),
            pltpu.VMEM((2, nc * nz * HW, ny), BF),
            pltpu.VMEM((2, nc, nx, 128), BF),
            pltpu.VMEM((2, nc, 16, 128), BF),
            pltpu.SemaphoreType.DMA((6,)),
            pltpu.SemaphoreType.DMA((6,)),
        ],
        compiler_params=pltpu.CompilerParams(
            collective_id=0, has_side_effects=True, vmem_limit_bytes=40 << 20
        ),
        name="halo",
    )(fields)
    payload = pl.pallas_call(
        functools.partial(tile_kernel, gxn, gyn, list_length),
        out_shape=jax.ShapeDtypeStruct((gxn, CAP * 16 + cells, 128), F32),
        in_specs=[SM, SM] + [VM] * 6,
        out_specs=VM,
        scratch_shapes=[
            pltpu.VMEM((SPAN // 4, nc * 48, 128), F32),
            pltpu.VMEM((144, SPAN * 32), BF),
            pltpu.VMEM((272, 2 * SPAN * 32), BF),
            pltpu.VMEM((HW, 2, 416, 128), F32),
            pltpu.VMEM((2, HW * 8 * TE, 128), F32),
            pltpu.VMEM((list_length * 16, 4096), BF),
            pltpu.VMEM((list_length * 16, 128), F32),
            pltpu.VMEM((cells, 16, 128), F32),
            pltpu.VMEM((cells, 8, 128), F32),
            pltpu.SMEM((gxn,), jnp.int32),
        ],
        compiler_params=pltpu.CompilerParams(vmem_limit_bytes=40 << 20),
        name="tiles",
    )(
        dense_list,
        filter_device,
        fields,
        edges,
        columns,
        corners,
        jnp.asarray(window_weights()),
        jnp.asarray(block_weights()),
    )
    got, every = pl.pallas_call(
        functools.partial(exchange_kernel, gxn, gyn),
        out_shape=(
            jax.ShapeDtypeStruct(payload.shape, F32),
            jax.ShapeDtypeStruct((gyn, gxn, cells, 128), F32),
        ),
        in_specs=[VM],
        out_specs=(VM, VM),
        scratch_shapes=[
            pltpu.VMEM((gxn, cells, 128), F32),
            pltpu.SemaphoreType.DMA((gxn,)),
            pltpu.SemaphoreType.DMA((gxn,)),
            pltpu.SemaphoreType.DMA((gyn,)),
            pltpu.SemaphoreType.DMA((gyn,)),
        ],
        compiler_params=pltpu.CompilerParams(collective_id=1, has_side_effects=True),
        name="exchange",
    )(payload)
    statistics, coarse = pl.pallas_call(
        functools.partial(select_kernel, gxn, gyn, list_length, cells_x),
        out_shape=(
            jax.ShapeDtypeStruct((per_filter, 2048), F32),
            jax.ShapeDtypeStruct((pencils // gyn, cells_x * gxn * HW * 8), F32),
        ),
        in_specs=[SM, SM, VM, VM],
        out_specs=(VM, VM),
        scratch_shapes=[pltpu.VMEM((per_filter, 16, 128), F32)],
        name="select",
    )(filter_device, pencil_order, got, every)
    return statistics, coarse


def solution(mesh):
    in_specs = (P(None, None, "gx", "gy"), P(), P(), P())
    out_specs = (P(("gx", "gy"), None), P("gy", None))
    body = functools.partial(shards, mesh.shape["gx"], mesh.shape["gy"])
    return jax.shard_map(
        body, mesh=mesh, in_specs=in_specs, out_specs=out_specs, check_vma=False
    )
```

```python
import functools

import jax
import jax.numpy as jnp
import numpy as np
from jax import lax
from jax.experimental import pallas as pl
from jax.experimental.pallas import tpu as pltpu
from jax.sharding import PartitionSpec as P

TE = 16
HW = 4
CAP = 2
SPAN = TE + 2 * HW
BF = jnp.bfloat16
F32 = jnp.float32
MESH = pl.DeviceIdType.MESH


def dot(a, b):
    return lax.dot_general(a, b, (((1,), (0,)), ((), ())), preferred_element_type=F32)


def window_weights():
    z = np.arange(SPAN)[:, None, None, None]
    w = np.arange(32)[None, :, None, None]
    zo = np.arange(TE)[None, None, :, None]
    yo = np.arange(TE)[None, None, None, :]
    out = []
    for k in range(1, HW + 1):
        m = (np.abs(z - HW - zo) <= k) & (np.abs(w - HW - yo) <= k)
        m = m.reshape(SPAN * 32, TE * TE)
        out.append(np.concatenate([m, m], axis=0))
    return np.stack(out).astype(jnp.bfloat16)


def block_weights():
    par = np.arange(2)[:, None, None, None]
    bx = np.arange(4)[None, :, None, None]
    h = np.arange(2)[None, None, :, None]
    lane = np.arange(128)[None, None, None, :]
    plane = h * 128 + lane
    target = par * 64 + (plane // TE // 4) * 16 + bx * 4 + (plane % TE) // 4
    target = target.reshape(-1)
    m = (target[:, None] == np.arange(128)[None, :]) / 64.0
    return np.concatenate([m, m], axis=0).astype(jnp.bfloat16)


def halo_kernel(gxn, gyn, f_ref, e_ref, yh_ref, yc_ref, col, sx, rx, sy, sc, ssem, rsem):
    nc, nz, nx, ny = f_ref.shape
    gx, gy = lax.axis_index("gx"), lax.axis_index("gy")
    right = (lax.rem(gx + 1, gxn), gy)
    left = (lax.rem(gx + gxn - 1, gxn), gy)
    up = (gx, lax.rem(gy + 1, gyn))
    down = (gx, lax.rem(gy + gyn - 1, gyn))
    barrier = pltpu.get_barrier_semaphore()
    for who in (left, right, up, down):
        pl.semaphore_signal(barrier, inc=1, device_id=who, device_id_type=MESH)
    hz = nz * HW

    def send(src, dst, sem, who):
        copy = pltpu.make_async_remote_copy(
            src_ref=src,
            dst_ref=dst,
            send_sem=ssem.at[sem],
            recv_sem=rsem.at[sem],
            device_id=who,
            device_id_type=MESH,
        )
        copy.start()
        return copy

    def pack(ref, lo):
        acc = None
        for j in range(nz // 2):
            lhs = jnp.concatenate(
                [ref[:, 2 * j + i, lo : lo + 16, :].reshape(nc * 16, ny) for i in range(2)],
                axis=1,
            )
            part = dot(lhs, col[j])
            acc = part if acc is None else acc + part
        return [
            acc[:, side * 128 : (side + 1) * 128].astype(BF).reshape(nc, 16, 128)
            for side in range(2)
        ]

    out = iota((hz, nz * 16), 0)
    put = iota((hz, nz * 16), 1)
    same = out // HW == put // 16
    pl.semaphore_wait(barrier, 4)
    xcopies = []
    for side, start, first, who in ((0, nx - 16, 16 - HW, right), (1, 0, 0, left)):
        take = one_hot(same & (put % 16 == first + out % HW))
        for c in range(nc):
            block = f_ref[c, :, start : start + 16, :].reshape(nz * 16, ny)
            sx[side, c * hz : (c + 1) * hz, :] = dot(take, block).astype(BF)
        xcopies.append(send(sx.at[side], rx.at[side], side, who))
    row = iota((2 * ny, 256), 0)
    lane = iota((2 * ny, 256), 1)
    y, l = row % ny, lane % 128
    spot = l - row // ny * HW
    low = jnp.where((lane < 128) & (y >= ny - HW), spot - y + (ny - HW), -1)
    base = jnp.where((lane >= 128) & (y < HW), spot - y, low)
    for j in range(nz // 2):
        col[j] = one_hot(base == 2 * HW * j)

    for part in range(nx // 16):
        both = pack(f_ref, part * 16)
        for side in range(2):
            sy[side, :, part * 16 : part * 16 + 16, :] = both[side]
    ycopies = [send(sy.at[0], yh_ref.at[0], 2, up), send(sy.at[1], yh_ref.at[1], 3, down)]
    put = iota((nz * 16, 2 * hz), 0)
    src = iota((nz * 16, 2 * hz), 1)
    code = put - put // 16 * 16
    inner = src % hz
    give = one_hot(
        (put // 16 == inner // HW)
        & (code == inner % HW + jnp.where(src < hz, 16 - HW, 0))
    )
    for copy in xcopies:
        copy.wait()
    for c in range(nc):
        rows = slice(c * hz, (c + 1) * hz)
        block = dot(give, jnp.concatenate([rx[0, rows, :], rx[1, rows, :]], axis=0))
        e_ref[c] = block.astype(BF).reshape(nz, 16, ny)
    both = pack(e_ref, 0)
    for side in range(2):
        sc[side] = both[side]
    ycopies.append(send(sc.at[0], yc_ref.at[0], 4, up))
    ycopies.append(send(sc.at[1], yc_ref.at[1], 5, down))
    for copy in ycopies:
        copy.wait()


def iota(shape, dim):
    return lax.broadcasted_iota(jnp.int32, shape, dim)


def one_hot(cond):
    return jnp.where(cond, 1.0, 0.0).astype(BF)


def tile_kernel(
    gxn,
    gyn,
    list_length,
    list_ref,
    target_ref,
    f_ref,
    e_ref,
    yh_ref,
    yc_ref,
    w_ref,
    m_ref,
    pay_ref,
    co_ref,
    t_ref,
    qp_ref,
    qm_ref,
    r_ref,
    c_ref,
    a_ref,
    s_ref,
    cell_ref,
    count_ref,
    used_ref,
):
    nc, nz, nx, ny = f_ref.shape
    across_x, across_y = nx // TE, ny // TE
    gx, gy = lax.axis_index("gx"), lax.axis_index("gy")
    total = jnp.int32(0)
    for e in range(list_length):
        total = total + jnp.where(target_ref[gy, gx, e] >= 0, 1, 0).astype(jnp.int32)
    quads = SPAN // 4

    @pl.loop(0, total)
    def _(t):
        tile = list_ref[gy, gx, t]
        tz = tile // (across_x * across_y)
        lx = tile // across_y % across_x
        ly = tile % across_y
        row = iota((4 * ny, 128), 0)
        col = iota((4 * ny, 128), 1)
        w = col % 32
        spread = one_hot(
            (row // ny == col // 32) & (w < SPAN) & (row % ny == ly * TE - HW + w)
        )
        x0 = pl.multiple_of(lx * TE, TE)
        x_low = pl.multiple_of(jnp.maximum(lx - 1, 0) * TE, TE)
        x_high = pl.multiple_of(jnp.minimum(lx + 1, across_x - 1) * TE, TE)

        def three(own, edge):
            low = jnp.where(lx == 0, edge, own(x_low))
            high = jnp.where(lx == across_x - 1, edge, own(x_high))
            return jnp.concatenate([low, own(x0), high], axis=1).reshape(nc * 48, 128)

        for j in range(quads):
            z0 = (tz * TE - HW + 4 * j + nz) % nz
            lhs = jnp.concatenate(
                [
                    three(lambda x, i=i: f_ref[:, z0 + i, pl.ds(x, 16), :], e_ref[:, z0 + i])
                    for i in range(4)
                ],
                axis=1,
            )
            t_ref[j] = dot(lhs, spread)

        @pl.when((ly == 0) | (ly == across_y - 1))
        def _():
            lhs = jnp.concatenate(
                [three(lambda x, i=i: yh_ref[i, :, pl.ds(x, 16), :], yc_ref[i]) for i in range(2)],
                axis=1,
            )
            lane = iota((256, 128), 0)
            out = iota((256, 128), 1)
            ww = out % 32
            for j in range(quads):
                z0 = (tz * TE - HW + 4 * j + nz) % nz
                source = (z0 + out // 32) * HW
                low = (ly == 0) & (ww < HW) & (lane == source + ww)
                high = (
                    (ly == across_y - 1)
                    & (ww >= SPAN - HW)
                    & (ww < SPAN)
                    & (lane == 128 + source + ww - (SPAN - HW))
                )
                t_ref[j] = t_ref[j] + dot(lhs, one_hot(low | high))

        for j in range(quads):
            lanes = slice(j * 128, (j + 1) * 128)
            lanes_low = slice((quads + j) * 128, (quads + j + 1) * 128)
            v = [t_ref[j, c * 48 + 12 : c * 48 + 36, :] for c in range(nc)]
            plain = [v[0], v[1], v[2], v[3], v[7], v[9]]
            for i in range(3):
                pair = jnp.concatenate(plain[2 * i : 2 * i + 2], axis=0)
                qp_ref[i * 48 : i * 48 + 48, lanes] = pair.astype(BF)
            prods = [v[0] * v[c] for c in (1, 2, 3, 4, 5, 6, 8, 7)]
            prods = prods + [v[9] * (v[1 + d] - v[4 + d]) for d in range(3)]
            for i in range(6):
                if i < 5:
                    pair = jnp.concatenate(prods[2 * i : 2 * i + 2], axis=0)
                else:
                    pair = jnp.concatenate([prods[10], jnp.zeros((8, 128), F32)], axis=0)
                rows = slice(i * 48, i * 48 + pair.shape[0])
                high = pair.astype(BF)
                qm_ref[rows, lanes] = high
                qm_ref[rows, lanes_low] = (pair - high.astype(F32)).astype(BF)
        for k in range(1, HW + 1):
            rp = dot(qp_ref[...], w_ref[k - 1, : SPAN * 32, :])
            rm = dot(qm_ref[...], w_ref[k - 1])
            scale = 1.0 / (2 * k + 1) ** 3
            for h in range(2):
                r_ref[k - 1, h, :144, :] = rp[:, h * 128 : (h + 1) * 128]
                r_ref[k - 1, h, 144:, :] = rm[:, h * 128 : (h + 1) * 128]
            for h in range(2):

                def f(q):
                    acc = None
                    for d in range(-k, k + 1):
                        start = q * SPAN + HW + d
                        part = r_ref[k - 1, h, start : start + TE, :]
                        acc = part if acc is None else acc + part
                    return acc

                inv = 1.0 / f(0)
                drag = f(5) * scale
                comps = [None] * 8
                for d in range(3):
                    ag = f(6 + d)
                    comps[d] = ag * inv - f(1 + d) * scale
                    comps[3 + d] = f(14 + d) * scale - drag * ((ag - f(9 + d)) * inv)
                comps[6] = f(12) * inv
                comps[7] = f(13) * inv - f(4) * scale
                for i in range(8):
                    at = ((k - 1) * 8 + i) * TE
                    c_ref[h, at : at + TE, :] = comps[i]
        where = pl.ds(pl.multiple_of(t * 16, 16), 16)
        for par in range(2):
            for bx in range(4):
                for h in range(2):
                    acc = None
                    for r in range(4):
                        part = c_ref[h, pl.ds(par * TE + bx * 4 + r, 16, stride=2 * TE), :]
                        acc = part if acc is None else acc + part
                    at = ((par * 4 + bx) * 2 + h) * 128
                    high = acc.astype(BF)
                    a_ref[where, at : at + 128] = high
                    a_ref[where, 2048 + at : 2048 + at + 128] = (
                        acc - high.astype(F32)
                    ).astype(BF)

    s_ref[...] = dot(a_ref[...], m_ref[...])
    cells = cell_ref.shape[0]
    cell_ref[...] = jnp.zeros(cell_ref.shape, F32)
    count_ref[...] = jnp.zeros(count_ref.shape, F32)
    for g in range(gxn):
        used_ref[g] = 0

    @pl.loop(0, total)
    def _(t):
        tile = list_ref[gy, gx, t]
        lx = tile // across_y % across_x
        ly = tile % across_y
        cell = (ly // 2) * (across_x // 2) + lx // 2
        target = target_ref[gy, gx, t]
        rank = used_ref[target]
        used_ref[target] = rank + 1
        stats = s_ref[pl.ds(pl.multiple_of(t * 16, 16), 16), :]
        pay_ref[target, pl.ds(pl.multiple_of(rank * 16, 16), 16), :] = stats
        cell_ref[cell] = cell_ref[cell] + stats
        count_ref[cell] = count_ref[cell] + 1.0

    lane = iota((16, 128), 1)
    row = iota((16, 128), 0)
    rows = []
    for cell in range(cells):
        sums = cell_ref[cell]
        even = jnp.sum(jnp.where(lane < 64, sums, 0.0), axis=1, keepdims=True)
        odd = jnp.sum(jnp.where(lane >= 64, sums, 0.0), axis=1, keepdims=True)
        spot = lane % 32
        placed = jnp.where(spot == 2 * row, even, jnp.where(spot == 2 * row + 1, odd, 0.0))
        sums = jnp.sum(placed, axis=0, keepdims=True) * (1.0 / 64.0)
        rows.append(sums / jnp.maximum(count_ref[cell, 0:1, :], 1.0))
    co_ref[...] = jnp.concatenate(rows, axis=0)


def exchange_kernel(
    gxn, gyn, pay_ref, co_ref, got_ref, all_ref, xs, xr, ys, yr, zs, zr
):
    gx, gy = lax.axis_index("gx"), lax.axis_index("gy")
    row_peers = [(lax.rem(gx + d, gxn), gy) for d in range(1, gxn)]
    column_peers = [(gx, lax.rem(gy + d, gyn)) for d in range(1, gyn)]
    barrier = pltpu.get_barrier_semaphore()
    for who in row_peers + column_peers:
        pl.semaphore_signal(barrier, inc=1, device_id=who, device_id_type=MESH)
    pl.semaphore_wait(barrier, gxn + gyn - 2)

    def send(src, dst, sends, receives, number, who):
        copy = pltpu.make_async_remote_copy(
            src_ref=src,
            dst_ref=dst,
            send_sem=sends.at[number],
            recv_sem=receives.at[number],
            device_id=who,
            device_id_type=MESH,
        )
        copy.start()
        return copy

    small = [
        send(co_ref, all_ref.at[gx, gy], ys, yr, n, who) for n, who in enumerate(column_peers)
    ]
    large = [
        send(pay_ref.at[who[0]], got_ref.at[gx], xs, xr, n, who)
        for n, who in enumerate(row_peers)
    ]
    all_ref[gx, gy] = co_ref[...]
    got_ref[gx] = pay_ref[gx]
    for copy in small:
        copy.wait()
    large = large + [
        send(all_ref.at[gx], all_ref.at[gx], zs, zr, n, who) for n, who in enumerate(row_peers)
    ]
    for copy in large:
        copy.wait()


def select_kernel(
    gxn, gyn, list_length, cells_x, target_ref, order_ref, got_ref, all_ref, o_ref, c_ref, held
):
    gx, gy = lax.axis_index("gx"), lax.axis_index("gy")

    spare = o_ref.shape[0]

    def source(s, slot):
        def entry(e, carry):
            slot, rank = carry
            hit = target_ref[gy, s, e] == gx
            at = pl.multiple_of(jnp.minimum(rank, CAP - 1) * 16, 16)
            held[jnp.where(hit, slot, spare)] = got_ref[s, pl.ds(at, 16), :]
            step = jnp.where(hit, 1, 0).astype(jnp.int32)
            return slot + step, rank + step

        return lax.fori_loop(0, list_length, entry, (slot, jnp.int32(0)), unroll=True)[0]

    lax.fori_loop(0, gxn, source, jnp.int32(0))
    for slot in range(o_ref.shape[0]):
        for r in range(16):
            o_ref[slot : slot + 1, r * 128 : (r + 1) * 128] = held[slot, r : r + 1, :]
    per_row = c_ref.shape[0]
    cells_y = all_ref.shape[2] // cells_x
    group = iota((1, 128), 1) // 32
    for r in range(per_row):
        pencil = order_ref[gy * per_row + r]
        owner = pencil // cells_y
        first = pencil % cells_y * cells_x
        for part in range(c_ref.shape[1] // 128):
            row = None
            for i in range(4):
                cx = part * 4 + i
                value = all_ref[cx // cells_x, owner, pl.ds(first + cx % cells_x, 1), :]
                row = value if row is None else jnp.where(group == i, value, row)
            c_ref[r : r + 1, part * 128 : (part + 1) * 128] = row


VM = pl.BlockSpec(memory_space=pltpu.VMEM)
SM = pl.BlockSpec(memory_space=pltpu.SMEM)


def shards(gxn, gyn, fields, dense_list, filter_device, pencil_order):
    nc, nz, nx, ny = fields.shape
    list_length = dense_list.shape[2]
    per_filter = gxn // 4 * (CAP + (CAP - 1) // 2)
    cells_x = nx // TE // 2
    cells = cells_x * (ny // TE // 2)
    pencils = pencil_order.shape[0]
    edges, columns, corners = pl.pallas_call(
        functools.partial(halo_kernel, gxn, gyn),
        out_shape=(
            jax.ShapeDtypeStruct((nc, nz, 16, ny), BF),
            jax.ShapeDtypeStruct((2, nc, nx, 128), BF),
            jax.ShapeDtypeStruct((2, nc, 16, 128), BF),
        ),
        in_specs=[VM],
        out_specs=(VM, VM, VM),
        scratch_shapes=[
            pltpu.VMEM((nz // 2, 2 * ny, 256), BF),
            pltpu.VMEM((2, nc * nz * HW, ny), BF),
            pltpu.VMEM((2, nc * nz * HW, ny), BF),
            pltpu.VMEM((2, nc, nx, 128), BF),
            pltpu.VMEM((2, nc, 16, 128), BF),
            pltpu.SemaphoreType.DMA((6,)),
            pltpu.SemaphoreType.DMA((6,)),
        ],
        compiler_params=pltpu.CompilerParams(
            collective_id=0, has_side_effects=True, vmem_limit_bytes=40 << 20
        ),
        name="halo",
    )(fields)
    payload, own_cells = pl.pallas_call(
        functools.partial(tile_kernel, gxn, gyn, list_length),
        out_shape=(
            jax.ShapeDtypeStruct((gxn, CAP * 16, 128), F32),
            jax.ShapeDtypeStruct((cells, 128), F32),
        ),
        in_specs=[SM, SM] + [VM] * 6,
        out_specs=(VM, VM),
        scratch_shapes=[
            pltpu.VMEM((SPAN // 4, nc * 48, 128), F32),
            pltpu.VMEM((144, SPAN * 32), BF),
            pltpu.VMEM((272, 2 * SPAN * 32), BF),
            pltpu.VMEM((HW, 2, 416, 128), F32),
            pltpu.VMEM((2, HW * 8 * TE, 128), F32),
            pltpu.VMEM((list_length * 16, 4096), BF),
            pltpu.VMEM((list_length * 16, 128), F32),
            pltpu.VMEM((cells, 16, 128), F32),
            pltpu.VMEM((cells, 8, 128), F32),
            pltpu.SMEM((gxn,), jnp.int32),
        ],
        compiler_params=pltpu.CompilerParams(vmem_limit_bytes=40 << 20),
        name="tiles",
    )(
        dense_list,
        filter_device,
        fields,
        edges,
        columns,
        corners,
        jnp.asarray(window_weights()),
        jnp.asarray(block_weights()),
    )
    got, every = pl.pallas_call(
        functools.partial(exchange_kernel, gxn, gyn),
        out_shape=(
            jax.ShapeDtypeStruct(payload.shape, F32),
            jax.ShapeDtypeStruct((gxn, gyn, cells, 128), F32),
        ),
        in_specs=[VM, VM],
        out_specs=(VM, VM),
        scratch_shapes=[
            pltpu.SemaphoreType.DMA((gxn - 1,)),
            pltpu.SemaphoreType.DMA((gxn - 1,)),
            pltpu.SemaphoreType.DMA((gyn - 1,)),
            pltpu.SemaphoreType.DMA((gyn - 1,)),
            pltpu.SemaphoreType.DMA((gxn - 1,)),
            pltpu.SemaphoreType.DMA((gxn - 1,)),
        ],
        compiler_params=pltpu.CompilerParams(collective_id=1, has_side_effects=True),
        name="exchange",
    )(payload, own_cells)
    statistics, coarse = pl.pallas_call(
        functools.partial(select_kernel, gxn, gyn, list_length, cells_x),
        out_shape=(
            jax.ShapeDtypeStruct((per_filter, 2048), F32),
            jax.ShapeDtypeStruct((pencils // gyn, cells_x * gxn * HW * 8), F32),
        ),
        in_specs=[SM, SM, VM, VM],
        out_specs=(VM, VM),
        scratch_shapes=[pltpu.VMEM((per_filter + 1, 16, 128), F32)],
        name="select",
    )(filter_device, pencil_order, got, every)
    return statistics, coarse


def solution(mesh):
    in_specs = (P(None, None, "gx", "gy"), P(), P(), P())
    out_specs = (P(("gx", "gy"), None), P("gy", None))
    body = functools.partial(shards, mesh.shape["gx"], mesh.shape["gy"])
    return jax.shard_map(
        body, mesh=mesh, in_specs=in_specs, out_specs=out_specs, check_vma=False
    )
```

```python
import functools

import jax
import jax.numpy as jnp
import numpy as np
from jax import lax
from jax.experimental import pallas as pl
from jax.experimental.pallas import tpu as pltpu
from jax.sharding import PartitionSpec as P

TE = 16
HW = 4
CAP = 2
SPAN = TE + 2 * HW
BF = jnp.bfloat16
F32 = jnp.float32
MESH = pl.DeviceIdType.MESH


def dot(a, b):
    return lax.dot_general(a, b, (((1,), (0,)), ((), ())), preferred_element_type=F32)


def window_weights():
    z = np.arange(SPAN)[:, None, None, None]
    w = np.arange(32)[None, :, None, None]
    zo = np.arange(TE)[None, None, :, None]
    yo = np.arange(TE)[None, None, None, :]
    out = []
    for k in range(1, HW + 1):
        m = (np.abs(z - HW - zo) <= k) & (np.abs(w - HW - yo) <= k)
        m = m.reshape(SPAN * 32, TE * TE)
        out.append(np.concatenate([m, m], axis=0))
    return np.stack(out).astype(jnp.bfloat16)


def block_weights():
    par = np.arange(2)[:, None, None, None]
    bx = np.arange(4)[None, :, None, None]
    h = np.arange(2)[None, None, :, None]
    lane = np.arange(128)[None, None, None, :]
    plane = h * 128 + lane
    target = par * 64 + (plane // TE // 4) * 16 + bx * 4 + (plane % TE) // 4
    target = target.reshape(-1)
    m = (target[:, None] == np.arange(128)[None, :]) / 64.0
    return np.concatenate([m, m], axis=0).astype(jnp.bfloat16)


def halo_kernel(gxn, gyn, f_ref, e_ref, yh_ref, yc_ref, col, sx, rx, sy, sc, ssem, rsem):
    nc, nz, nx, ny = f_ref.shape
    gx, gy = lax.axis_index("gx"), lax.axis_index("gy")
    right = (lax.rem(gx + 1, gxn), gy)
    left = (lax.rem(gx + gxn - 1, gxn), gy)
    up = (gx, lax.rem(gy + 1, gyn))
    down = (gx, lax.rem(gy + gyn - 1, gyn))
    barrier = pltpu.get_barrier_semaphore()
    for who in (left, right, up, down):
        pl.semaphore_signal(barrier, inc=1, device_id=who, device_id_type=MESH)
    hz = nz * HW

    def send(src, dst, sem, who):
        copy = pltpu.make_async_remote_copy(
            src_ref=src,
            dst_ref=dst,
            send_sem=ssem.at[sem],
            recv_sem=rsem.at[sem],
            device_id=who,
            device_id_type=MESH,
        )
        copy.start()
        return copy

    def pack(ref, lo, rows):
        acc = None
        for j in range(nz // 2):
            lhs = jnp.concatenate(
                [ref[:, 2 * j + i, lo : lo + rows, :].reshape(nc * rows, ny) for i in range(2)],
                axis=1,
            )
            part = dot(lhs, col[j])
            acc = part if acc is None else acc + part
        return [
            acc[:, side * 128 : (side + 1) * 128].astype(BF).reshape(nc, rows, 128)
            for side in range(2)
        ]

    out = iota((hz, nz * 16), 0)
    put = iota((hz, nz * 16), 1)
    same = out // HW == put // 16
    pl.semaphore_wait(barrier, 4)
    xcopies = []
    for side, start, first, who in ((0, nx - 16, 16 - HW, right), (1, 0, 0, left)):
        take = one_hot(same & (put % 16 == first + out % HW))
        for c in range(nc):
            block = f_ref[c, :, start : start + 16, :].reshape(nz * 16, ny)
            sx[side, c * hz : (c + 1) * hz, :] = dot(take, block).astype(BF)
        xcopies.append(send(sx.at[side], rx.at[side], side, who))
    row = iota((2 * ny, 256), 0)
    lane = iota((2 * ny, 256), 1)
    y, l = row % ny, lane % 128
    spot = l - row // ny * HW
    low = jnp.where((lane < 128) & (y >= ny - HW), spot - y + (ny - HW), -1)
    base = jnp.where((lane >= 128) & (y < HW), spot - y, low)
    for j in range(nz // 2):
        col[j] = one_hot(base == 2 * HW * j)

    for part in range(nx // 32):
        both = pack(f_ref, part * 32, 32)
        for side in range(2):
            sy[side, :, part * 32 : part * 32 + 32, :] = both[side]
    ycopies = [send(sy.at[0], yh_ref.at[0], 2, up), send(sy.at[1], yh_ref.at[1], 3, down)]
    put = iota((nz * 16, 2 * hz), 0)
    src = iota((nz * 16, 2 * hz), 1)
    code = put - put // 16 * 16
    inner = src % hz
    give = one_hot(
        (put // 16 == inner // HW)
        & (code == inner % HW + jnp.where(src < hz, 16 - HW, 0))
    )
    for copy in xcopies:
        copy.wait()
    for c in range(nc):
        rows = slice(c * hz, (c + 1) * hz)
        block = dot(give, jnp.concatenate([rx[0, rows, :], rx[1, rows, :]], axis=0))
        e_ref[c] = block.astype(BF).reshape(nz, 16, ny)
    both = pack(e_ref, 0, 16)
    for side in range(2):
        sc[side] = both[side]
    ycopies.append(send(sc.at[0], yc_ref.at[0], 4, up))
    ycopies.append(send(sc.at[1], yc_ref.at[1], 5, down))
    for copy in ycopies:
        copy.wait()


def iota(shape, dim):
    return lax.broadcasted_iota(jnp.int32, shape, dim)


def one_hot(cond):
    return jnp.where(cond, 1.0, 0.0).astype(BF)


def tile_kernel(
    gxn,
    gyn,
    list_length,
    list_ref,
    target_ref,
    f_ref,
    e_ref,
    yh_ref,
    yc_ref,
    w_ref,
    m_ref,
    pay_ref,
    co_ref,
    t_ref,
    qp_ref,
    qm_ref,
    r_ref,
    c_ref,
    a_ref,
    s_ref,
    cell_ref,
    count_ref,
    used_ref,
):
    nc, nz, nx, ny = f_ref.shape
    across_x, across_y = nx // TE, ny // TE
    gx, gy = lax.axis_index("gx"), lax.axis_index("gy")
    total = jnp.int32(0)
    for e in range(list_length):
        total = total + jnp.where(target_ref[gy, gx, e] >= 0, 1, 0).astype(jnp.int32)
    quads = SPAN // 4

    @pl.loop(0, total)
    def _(t):
        tile = list_ref[gy, gx, t]
        tz = tile // (across_x * across_y)
        lx = tile // across_y % across_x
        ly = tile % across_y
        row = iota((4 * ny, 128), 0)
        col = iota((4 * ny, 128), 1)
        w = col % 32
        spread = one_hot(
            (row // ny == col // 32) & (w < SPAN) & (row % ny == ly * TE - HW + w)
        )
        x0 = pl.multiple_of(lx * TE, TE)
        x_low = pl.multiple_of(jnp.maximum(lx - 1, 0) * TE, TE)
        x_high = pl.multiple_of(jnp.minimum(lx + 1, across_x - 1) * TE, TE)

        def three(own, edge):
            low = jnp.where(lx == 0, edge, own(x_low))
            high = jnp.where(lx == across_x - 1, edge, own(x_high))
            return jnp.concatenate([low, own(x0), high], axis=1).reshape(nc * 48, 128)

        for j in range(quads):
            z0 = (tz * TE - HW + 4 * j + nz) % nz
            lhs = jnp.concatenate(
                [
                    three(lambda x, i=i: f_ref[:, z0 + i, pl.ds(x, 16), :], e_ref[:, z0 + i])
                    for i in range(4)
                ],
                axis=1,
            )
            t_ref[j] = dot(lhs, spread)

        @pl.when((ly == 0) | (ly == across_y - 1))
        def _():
            lhs = jnp.concatenate(
                [three(lambda x, i=i: yh_ref[i, :, pl.ds(x, 16), :], yc_ref[i]) for i in range(2)],
                axis=1,
            )
            lane = iota((256, 128), 0)
            out = iota((256, 128), 1)
            ww = out % 32
            for j in range(quads):
                z0 = (tz * TE - HW + 4 * j + nz) % nz
                source = (z0 + out // 32) * HW
                low = (ly == 0) & (ww < HW) & (lane == source + ww)
                high = (
                    (ly == across_y - 1)
                    & (ww >= SPAN - HW)
                    & (ww < SPAN)
                    & (lane == 128 + source + ww - (SPAN - HW))
                )
                t_ref[j] = t_ref[j] + dot(lhs, one_hot(low | high))

        for j in range(quads):
            lanes = slice(j * 128, (j + 1) * 128)
            lanes_low = slice((quads + j) * 128, (quads + j + 1) * 128)
            v = [t_ref[j, c * 48 + 12 : c * 48 + 36, :] for c in range(nc)]
            plain = [v[0], v[1], v[2], v[3], v[7], v[9]]
            for i in range(3):
                pair = jnp.concatenate(plain[2 * i : 2 * i + 2], axis=0)
                qp_ref[i * 48 : i * 48 + 48, lanes] = pair.astype(BF)
            prods = [v[0] * v[c] for c in (1, 2, 3, 4, 5, 6, 8, 7)]
            prods = prods + [v[9] * (v[1 + d] - v[4 + d]) for d in range(3)]
            for i in range(6):
                if i < 5:
                    pair = jnp.concatenate(prods[2 * i : 2 * i + 2], axis=0)
                else:
                    pair = jnp.concatenate([prods[10], jnp.zeros((8, 128), F32)], axis=0)
                rows = slice(i * 48, i * 48 + pair.shape[0])
                high = pair.astype(BF)
                qm_ref[rows, lanes] = high
                qm_ref[rows, lanes_low] = (pair - high.astype(F32)).astype(BF)
        for k in range(1, HW + 1):
            rp = dot(qp_ref[...], w_ref[k - 1, : SPAN * 32, :])
            rm = dot(qm_ref[...], w_ref[k - 1])
            scale = 1.0 / (2 * k + 1) ** 3
            for h in range(2):
                r_ref[k - 1, h, :144, :] = rp[:, h * 128 : (h + 1) * 128]
                r_ref[k - 1, h, 144:, :] = rm[:, h * 128 : (h + 1) * 128]
            for h in range(2):

                def f(q):
                    acc = None
                    for d in range(-k, k + 1):
                        start = q * SPAN + HW + d
                        part = r_ref[k - 1, h, start : start + TE, :]
                        acc = part if acc is None else acc + part
                    return acc

                inv = 1.0 / f(0)
                drag = f(5) * scale
                comps = [None] * 8
                for d in range(3):
                    ag = f(6 + d)
                    comps[d] = ag * inv - f(1 + d) * scale
                    comps[3 + d] = f(14 + d) * scale - drag * ((ag - f(9 + d)) * inv)
                comps[6] = f(12) * inv
                comps[7] = f(13) * inv - f(4) * scale
                for i in range(8):
                    at = ((k - 1) * 8 + i) * TE
                    c_ref[h, at : at + TE, :] = comps[i]
        where = pl.ds(pl.multiple_of(t * 16, 16), 16)
        for par in range(2):
            for bx in range(4):
                for h in range(2):
                    acc = None
                    for r in range(4):
                        part = c_ref[h, pl.ds(par * TE + bx * 4 + r, 16, stride=2 * TE), :]
                        acc = part if acc is None else acc + part
                    at = ((par * 4 + bx) * 2 + h) * 128
                    high = acc.astype(BF)
                    a_ref[where, at : at + 128] = high
                    a_ref[where, 2048 + at : 2048 + at + 128] = (
                        acc - high.astype(F32)
                    ).astype(BF)

    s_ref[...] = dot(a_ref[...], m_ref[...])
    cells = cell_ref.shape[0]
    cell_ref[...] = jnp.zeros(cell_ref.shape, F32)
    count_ref[...] = jnp.zeros(count_ref.shape, F32)
    for g in range(gxn):
        used_ref[g] = 0

    @pl.loop(0, total)
    def _(t):
        tile = list_ref[gy, gx, t]
        lx = tile // across_y % across_x
        ly = tile % across_y
        cell = (ly // 2) * (across_x // 2) + lx // 2
        target = target_ref[gy, gx, t]
        rank = used_ref[target]
        used_ref[target] = rank + 1
        stats = s_ref[pl.ds(pl.multiple_of(t * 16, 16), 16), :]
        pay_ref[target, pl.ds(pl.multiple_of(rank * 16, 16), 16), :] = stats
        cell_ref[cell] = cell_ref[cell] + stats
        count_ref[cell] = count_ref[cell] + 1.0

    lane = iota((16, 128), 1)
    row = iota((16, 128), 0)
    rows = []
    for cell in range(cells):
        sums = cell_ref[cell]
        even = jnp.sum(jnp.where(lane < 64, sums, 0.0), axis=1, keepdims=True)
        odd = jnp.sum(jnp.where(lane >= 64, sums, 0.0), axis=1, keepdims=True)
        spot = lane % 32
        placed = jnp.where(spot == 2 * row, even, jnp.where(spot == 2 * row + 1, odd, 0.0))
        sums = jnp.sum(placed, axis=0, keepdims=True) * (1.0 / 64.0)
        rows.append(sums / jnp.maximum(count_ref[cell, 0:1, :], 1.0))
    co_ref[...] = jnp.concatenate(rows, axis=0)


def exchange_kernel(
    gxn, gyn, pay_ref, co_ref, got_ref, all_ref, xs, xr, ys, yr, zs, zr
):
    gx, gy = lax.axis_index("gx"), lax.axis_index("gy")
    row_peers = [(lax.rem(gx + d, gxn), gy) for d in range(1, gxn)]
    column_peers = [(gx, lax.rem(gy + d, gyn)) for d in range(1, gyn)]
    barrier = pltpu.get_barrier_semaphore()
    for who in row_peers + column_peers:
        pl.semaphore_signal(barrier, inc=1, device_id=who, device_id_type=MESH)
    pl.semaphore_wait(barrier, gxn + gyn - 2)

    def send(src, dst, sends, receives, number, who):
        copy = pltpu.make_async_remote_copy(
            src_ref=src,
            dst_ref=dst,
            send_sem=sends.at[number],
            recv_sem=receives.at[number],
            device_id=who,
            device_id_type=MESH,
        )
        copy.start()
        return copy

    small = [
        send(co_ref, all_ref.at[gx, gy], ys, yr, n, who) for n, who in enumerate(column_peers)
    ]
    large = [
        send(pay_ref.at[who[0]], got_ref.at[gx], xs, xr, n, who)
        for n, who in enumerate(row_peers)
    ]
    all_ref[gx, gy] = co_ref[...]
    got_ref[gx] = pay_ref[gx]
    for copy in small:
        copy.wait()
    large = large + [
        send(all_ref.at[gx], all_ref.at[gx], zs, zr, n, who) for n, who in enumerate(row_peers)
    ]
    for copy in large:
        copy.wait()


def select_kernel(
    gxn, gyn, list_length, cells_x, target_ref, order_ref, got_ref, all_ref, o_ref, c_ref, held
):
    gx, gy = lax.axis_index("gx"), lax.axis_index("gy")

    spare = o_ref.shape[0]

    def source(s, slot):
        def entry(e, carry):
            slot, rank = carry
            hit = target_ref[gy, s, e] == gx
            at = pl.multiple_of(jnp.minimum(rank, CAP - 1) * 16, 16)
            held[jnp.where(hit, slot, spare)] = got_ref[s, pl.ds(at, 16), :]
            step = jnp.where(hit, 1, 0).astype(jnp.int32)
            return slot + step, rank + step

        return lax.fori_loop(0, list_length, entry, (slot, jnp.int32(0)), unroll=True)[0]

    lax.fori_loop(0, gxn, source, jnp.int32(0))
    for slot in range(o_ref.shape[0]):
        for r in range(16):
            o_ref[slot : slot + 1, r * 128 : (r + 1) * 128] = held[slot, r : r + 1, :]
    per_row = c_ref.shape[0]
    cells_y = all_ref.shape[2] // cells_x
    group = iota((1, 128), 1) // 32
    for r in range(per_row):
        pencil = order_ref[gy * per_row + r]
        owner = pencil // cells_y
        first = pencil % cells_y * cells_x
        for part in range(c_ref.shape[1] // 128):
            row = None
            for i in range(4):
                cx = part * 4 + i
                value = all_ref[cx // cells_x, owner, pl.ds(first + cx % cells_x, 1), :]
                row = value if row is None else jnp.where(group == i, value, row)
            c_ref[r : r + 1, part * 128 : (part + 1) * 128] = row


VM = pl.BlockSpec(memory_space=pltpu.VMEM)
SM = pl.BlockSpec(memory_space=pltpu.SMEM)


def shards(gxn, gyn, fields, dense_list, filter_device, pencil_order):
    nc, nz, nx, ny = fields.shape
    list_length = dense_list.shape[2]
    per_filter = gxn // 4 * (CAP + (CAP - 1) // 2)
    cells_x = nx // TE // 2
    cells = cells_x * (ny // TE // 2)
    pencils = pencil_order.shape[0]
    edges, columns, corners = pl.pallas_call(
        functools.partial(halo_kernel, gxn, gyn),
        out_shape=(
            jax.ShapeDtypeStruct((nc, nz, 16, ny), BF),
            jax.ShapeDtypeStruct((2, nc, nx, 128), BF),
            jax.ShapeDtypeStruct((2, nc, 16, 128), BF),
        ),
        in_specs=[VM],
        out_specs=(VM, VM, VM),
        scratch_shapes=[
            pltpu.VMEM((nz // 2, 2 * ny, 256), BF),
            pltpu.VMEM((2, nc * nz * HW, ny), BF),
            pltpu.VMEM((2, nc * nz * HW, ny), BF),
            pltpu.VMEM((2, nc, nx, 128), BF),
            pltpu.VMEM((2, nc, 16, 128), BF),
            pltpu.SemaphoreType.DMA((6,)),
            pltpu.SemaphoreType.DMA((6,)),
        ],
        compiler_params=pltpu.CompilerParams(
            collective_id=0, has_side_effects=True, vmem_limit_bytes=40 << 20
        ),
        name="halo",
    )(fields)
    payload, own_cells = pl.pallas_call(
        functools.partial(tile_kernel, gxn, gyn, list_length),
        out_shape=(
            jax.ShapeDtypeStruct((gxn, CAP * 16, 128), F32),
            jax.ShapeDtypeStruct((cells, 128), F32),
        ),
        in_specs=[SM, SM] + [VM] * 6,
        out_specs=(VM, VM),
        scratch_shapes=[
            pltpu.VMEM((SPAN // 4, nc * 48, 128), F32),
            pltpu.VMEM((144, SPAN * 32), BF),
            pltpu.VMEM((272, 2 * SPAN * 32), BF),
            pltpu.VMEM((HW, 2, 416, 128), F32),
            pltpu.VMEM((2, HW * 8 * TE, 128), F32),
            pltpu.VMEM((list_length * 16, 4096), BF),
            pltpu.VMEM((list_length * 16, 128), F32),
            pltpu.VMEM((cells, 16, 128), F32),
            pltpu.VMEM((cells, 8, 128), F32),
            pltpu.SMEM((gxn,), jnp.int32),
        ],
        compiler_params=pltpu.CompilerParams(vmem_limit_bytes=40 << 20),
        name="tiles",
    )(
        dense_list,
        filter_device,
        fields,
        edges,
        columns,
        corners,
        jnp.asarray(window_weights()),
        jnp.asarray(block_weights()),
    )
    got, every = pl.pallas_call(
        functools.partial(exchange_kernel, gxn, gyn),
        out_shape=(
            jax.ShapeDtypeStruct(payload.shape, F32),
            jax.ShapeDtypeStruct((gxn, gyn, cells, 128), F32),
        ),
        in_specs=[VM, VM],
        out_specs=(VM, VM),
        scratch_shapes=[
            pltpu.SemaphoreType.DMA((gxn - 1,)),
            pltpu.SemaphoreType.DMA((gxn - 1,)),
            pltpu.SemaphoreType.DMA((gyn - 1,)),
            pltpu.SemaphoreType.DMA((gyn - 1,)),
            pltpu.SemaphoreType.DMA((gxn - 1,)),
            pltpu.SemaphoreType.DMA((gxn - 1,)),
        ],
        compiler_params=pltpu.CompilerParams(collective_id=1, has_side_effects=True),
        name="exchange",
    )(payload, own_cells)
    statistics, coarse = pl.pallas_call(
        functools.partial(select_kernel, gxn, gyn, list_length, cells_x),
        out_shape=(
            jax.ShapeDtypeStruct((per_filter, 2048), F32),
            jax.ShapeDtypeStruct((pencils // gyn, cells_x * gxn * HW * 8), F32),
        ),
        in_specs=[SM, SM, VM, VM],
        out_specs=(VM, VM),
        scratch_shapes=[pltpu.VMEM((per_filter + 1, 16, 128), F32)],
        name="select",
    )(filter_device, pencil_order, got, every)
    return statistics, coarse


def solution(mesh):
    in_specs = (P(None, None, "gx", "gy"), P(), P(), P())
    out_specs = (P(("gx", "gy"), None), P("gy", None))
    body = functools.partial(shards, mesh.shape["gx"], mesh.shape["gy"])
    return jax.shard_map(
        body, mesh=mesh, in_specs=in_specs, out_specs=out_specs, check_vma=False
    )
```
